32 devices in a mesh: groups: 2 (over x), table: 16 (over z, y, core).
Axes of the slice: x: 2, y: 2, z: 4, core: 2. Of those that a mesh axis runs over, the one named last changes fastest.
Arguments:
- hidden: bfloat16 [8192, 2560], P(('groups', 'table')), parts along dimension 0, may hold values from -6 to 6
- cotangent: bfloat16 [8192, 2560], P(('groups', 'table')), parts along dimension 0, may hold values from -6 to 6
- row_owner: int32 [8192, 8], P(('groups', 'table')), parts along dimension 0, may hold values from 0 to 15, all different within a row; in each aligned block of 256 rows (0 to 255, 256 to 511, ...) at most 256 rows name the same one
- row_slot: int32 [8192, 8], P(('groups', 'table')), parts along dimension 0, may hold values from 0 to 9215
- ngram_table: bfloat16 [147456, 160], P('table'), may hold values from -6 to 6
- w_key: bfloat16 [1280, 2560], P('table'), may hold values from -0.15625 to 0.15625
- w_value: bfloat16 [1280, 2560], P('table'), may hold values from -0.15625 to 0.15625
- conv_weight: float32 [4, 2560], replicated, may hold values from -3 to 3
Outputs:
- layer_out: bfloat16 [8192, 2560], P(('groups', 'table')), parts along dimension 0
- hidden_grad: bfloat16 [8192, 2560], P(('groups', 'table')), parts along dimension 0
- table_grad: bfloat16 [294912, 160], P(('groups', 'table')), parts along dimension 0
The draws below stay inside these ranges and needn't reach their ends.
There are 2 independent parts, one for each index of `groups`. The reference program is written for one: setup_inputs(seed, part) draws one part's arguments, and reference() takes and returns one part's arrays. A program takes and returns all parts, laid end to end along the dimension named above; an argument that names none is the same for every part. Nothing has to cross between parts.
Inputs may be any that keep to these rules, and one draw needn't show every extreme that they name: `row_owner`: owner devices of a token's 8 heads differ; among the rows of one device no owner is named more than 256 times, and in some devices one owner is named exactly 256 times.
All inputs are finite; a program needn't handle non-finite values.
Results may differ from the reference program's by a relative error of at most 0.0054.
Values may be sent and summed in bfloat16 or wider, within the bound.
A program may use at most 128 MiB of HBM per device.

```python
import math
import jax
import jax.numpy as jnp
import numpy as np
from jax import lax

D = 2560
HEADS = 8
HW = 160
MEM = 1280
ROWS_PER_DEVICE = 9216
ROWS = 147456
TOK_DEV = 256
TOKENS = 4096
LENGTH = 4096
KW = 4
MAX_GRAM_ORDER = 3
CAP = 256
N_TABLE = 16


def plant(result, stream_key, smallest, top_value):
    index_at = [jax.random.randint(jax.random.fold_in(stream_key, axis), (), 0, length) for axis, length in enumerate(result.shape)]
    main_axis = result.shape.index(max(result.shape))
    neighbour = index_at[:main_axis] + [(index_at[main_axis] + 1) % result.shape[main_axis]] + index_at[main_axis + 1:]
    return result.at[tuple(index_at)].set(smallest).at[tuple(neighbour)].set(top_value)


def levels(stream_key, dims, cuts, least, high):
    factor_of, own = 1.0, jax.random.fold_in(stream_key, 6)
    for dim, shards_of in cuts:
        steps = jnp.exp(jax.random.uniform(jax.random.fold_in(own, dim), (shards_of,), jnp.float32, least / len(cuts), high / len(cuts)))
        factor_of = factor_of * jnp.repeat(steps, dims[dim] // shards_of).reshape([-1 if axis == dim else 1 for axis in range(len(dims))])
    return factor_of


def shared_out(rng, own, number, rows, number_of, top, bound, skew):
    order = jax.random.permutation(rng, number_of)
    crowded, usual = load_shares(number_of, rows * top, bound, skew, True), load_shares(number_of, rows * top, bound, skew, False)
    places = jnp.arange(number_of)

    def named(tallies, turn):
        used = int((tallies > 0).sum())
        fixed = max(1, used // 4)
        passed = fixed + (places - fixed + turn * (used - fixed)) % max(1, number_of - fixed)
        return jnp.zeros((number_of,), jnp.int32).at[order[jnp.where(places < fixed, places, passed)]].set(jnp.asarray(tallies, jnp.int32))

    tallies = jnp.where(number % 4 == 0, named(crowded, number // 4), named(usual, number - number // 4 - 1))
    mixed = jax.random.permutation(jax.random.fold_in(own, 3), number_of)
    donor, taker = mixed[0:number_of // 2 * 2:2], mixed[1:number_of // 2 * 2:2]
    slack = jnp.minimum(tallies[donor] - 1, bound - tallies[taker]) // 2
    slack = jnp.where((donor == order[0]) | (taker == order[0]) | (tallies[taker] == 0), 0, jnp.maximum(slack, 0))
    passed = jax.random.randint(jax.random.fold_in(own, 4), (number_of // 2,), 0, 1 << 20) % (slack + 1)
    tallies = tallies.at[donor].add(-passed).at[taker].add(passed)
    members = jnp.searchsorted(jnp.cumsum(tallies), jnp.arange(rows * top), side="right").astype(jnp.int32)
    table = members.reshape(top, rows).T
    table = table[jax.random.permutation(jax.random.fold_in(own, 1), rows)]
    turn = jax.random.randint(jax.random.fold_in(own, 2), (rows, 1), 0, top)
    return jnp.take_along_axis(table, (jnp.arange(top)[None, :] + turn) % top, axis=1)


def load_shares(count, total, reach, lean, full):
    weights = [(1 << 20) // math.isqrt(grade ** lean) + 1 for grade in range(1, count + 1)]
    largest = reach if full else min(reach, max(-(-total // count), total * weights[0] // sum(weights)))
    least = 1 if total - largest >= count - 1 else 0
    given, spare = [largest] + [least] * (count - 1), total - largest - least * (count - 1)
    while spare > 0:
        free = [i for i in range(1, count) if given[i] < largest] or [i for i in range(1, count) if given[i] < reach]
        pool, remaining = sum([weights[i] for i in free]), spare
        for i in free:
            extra = min(reach - given[i], max(1, remaining * weights[i] // pool), spare)
            given[i] = given[i] + extra
            spare = spare - extra
    return np.array(given)


def gaussian(rng, extent, deviation, reach, split=(), kind=jnp.bfloat16):
    result = deviation * jax.random.normal(rng, extent, jnp.float32)
    if split:
        result = result * levels(rng, extent, split, -0.22, 0.18)
    return jnp.clip(result, -reach, reach).astype(kind)


def setup_inputs(seed: int = 0, part: int = 0) -> dict:
    streams_of = jax.random.split(jax.random.key(seed), 9)
    own_keys = jax.random.split(jax.random.fold_in(streams_of[8], part), 9)
    hidden = gaussian(own_keys[0], (TOKENS, D), 1.0, 6.0, ((0, 16),))
    cotangent = gaussian(own_keys[1], (TOKENS, D), 1.0, 6.0, ((0, 16),))
    row_owner_keys = jax.random.split(jax.random.fold_in(own_keys[2], 1), TOKENS // TOK_DEV)
    row_owner_turns = jax.random.permutation(jax.random.fold_in(own_keys[2], 3), TOKENS // TOK_DEV)
    row_owner = jax.vmap(lambda own, number: shared_out(jax.random.fold_in(own_keys[2], 2), own, number, TOK_DEV, N_TABLE, HEADS, CAP, 2))(row_owner_keys, row_owner_turns).reshape((TOKENS, HEADS))
    row_slot = plant(jax.random.randint(own_keys[3], (TOKENS, HEADS), 0, ROWS_PER_DEVICE), jax.random.fold_in(own_keys[3], 1), 0, ROWS_PER_DEVICE - 1).astype(jnp.int32)
    ngram_table = gaussian(streams_of[4], (ROWS, HW), 1.0, 6.0, ((0, 16),))
    w_key = gaussian(streams_of[5], (MEM, D), MEM ** -0.5, 0.15625, ((0, 16),))
    w_value = gaussian(streams_of[6], (MEM, D), MEM ** -0.5, 0.15625, ((0, 16),))
    conv_weight = gaussian(streams_of[7], (KW, D), 0.5, 3.0, (), jnp.float32)
    return dict(hidden=hidden, cotangent=cotangent, row_owner=row_owner, row_slot=row_slot, ngram_table=ngram_table, w_key=w_key, w_value=w_value, conv_weight=conv_weight)


epsilon = 1e-06

def inverse_rms(values):
    return lax.rsqrt(lax.optimization_barrier(jnp.mean(values * values, axis=-1, keepdims=True)) + epsilon)

def reference(hidden, cotangent, row_owner, row_slot, ngram_table, w_key, w_value, conv_weight):
    total = hidden.shape[0]
    row_ids = (row_owner * ROWS_PER_DEVICE + row_slot).astype(jnp.int32)
    memory = ngram_table[row_ids].reshape(total, HEADS * HW)
    keys_proj = jnp.dot(memory, w_key, preferred_element_type=jnp.float32)
    values_proj = jnp.dot(memory, w_value, preferred_element_type=jnp.float32)
    hidden_f = hidden.astype(jnp.float32)
    hidden_scale_factor = inverse_rms(hidden_f)
    scale_keys = inverse_rms(keys_proj)
    hidden_n = hidden_f * hidden_scale_factor
    keys_n = keys_proj * scale_keys
    root_width = math.sqrt(D)
    score = lax.optimization_barrier(jnp.sum(hidden_n * keys_n, axis=-1, keepdims=True)) / root_width
    gate = jax.nn.sigmoid(score)
    gated = gate * values_proj
    scale_gated = inverse_rms(gated)
    normed = (gated * scale_gated).astype(jnp.bfloat16)
    position = jnp.arange(total) % LENGTH
    mixed = jnp.zeros((total, D), jnp.float32)
    for kernel_tap_index in range(KW):
        start_offset = kernel_tap_index * MAX_GRAM_ORDER
        moved = jnp.concatenate([jnp.zeros((start_offset, D), jnp.bfloat16), normed[:total - start_offset]], axis=0).astype(jnp.float32)
        mixed = mixed + conv_weight[kernel_tap_index] * jnp.where((position >= start_offset)[:, None], moved, 0.0)
    layer_out = (jax.nn.silu(mixed) + gated).astype(jnp.bfloat16)
    upstream = cotangent.astype(jnp.float32)
    sigm = jax.nn.sigmoid(mixed)
    slope = upstream * sigm * (1.0 + mixed * (1.0 - sigm))
    normed_grad = jnp.zeros((total, D), jnp.float32)
    for kernel_tap_index in range(KW):
        start_offset = kernel_tap_index * MAX_GRAM_ORDER
        moved = jnp.concatenate([slope[start_offset:], jnp.zeros((start_offset, D), jnp.float32)], axis=0)
        normed_grad = normed_grad + conv_weight[kernel_tap_index] * jnp.where((position + start_offset < LENGTH)[:, None], moved, 0.0)
    gated_grad = upstream + scale_gated * normed_grad - scale_gated ** 3 * gated * lax.optimization_barrier(jnp.sum(normed_grad * gated, axis=-1, keepdims=True)) / D
    values_grad = (gate * gated_grad).astype(jnp.bfloat16)
    score_grad = lax.optimization_barrier(jnp.sum(gated_grad * values_proj, axis=-1, keepdims=True)) * gate * (1.0 - gate)
    keys_n_grad = score_grad * hidden_n / root_width
    hidden_n_grad = score_grad * keys_n / root_width
    keys_grad = (scale_keys * keys_n_grad - scale_keys ** 3 * keys_proj * lax.optimization_barrier(jnp.sum(keys_n_grad * keys_proj, axis=-1, keepdims=True)) / D).astype(jnp.bfloat16)
    hidden_grad = (hidden_scale_factor * hidden_n_grad - hidden_scale_factor ** 3 * hidden_f * lax.optimization_barrier(jnp.sum(hidden_n_grad * hidden_f, axis=-1, keepdims=True)) / D).astype(jnp.bfloat16)
    memory_grad = (jnp.dot(keys_grad, w_key.T, preferred_element_type=jnp.float32) + jnp.dot(values_grad, w_value.T, preferred_element_type=jnp.float32)).astype(jnp.bfloat16)
    table_sum = jnp.zeros((ROWS_PER_DEVICE * N_TABLE, HW), jnp.float32).at[row_ids.reshape(-1)].add(memory_grad.reshape(-1, HW).astype(jnp.float32))
    return (layer_out, hidden_grad, table_sum.astype(jnp.bfloat16))
```

```python
import functools
import math

import jax
import jax.numpy as jnp
from jax import lax
from jax.experimental import pallas as pl
from jax.experimental.pallas import tpu as pltpu
from jax.sharding import PartitionSpec as P

LENGTH = 4096
MAX_GRAM_ORDER = 3


epsilon = 1e-06


def shifted(value, axis, by):
    peers = lax.axis_size(axis)
    pairs = [(i, i + by) for i in range(peers) if 0 <= i + by < peers]
    return lax.ppermute(value, axis, pairs)


def inverse_rms(values):
    return lax.rsqrt(jnp.mean(values * values, axis=-1, keepdims=True) + epsilon)


def contract_last(left, right):
    return lax.dot_general(
        left, right, (((1,), (1,)), ((), ())), preferred_element_type=jnp.float32
    )


def contract_first(left, right):
    return lax.dot_general(
        left, right, (((0,), (0,)), ((), ())), preferred_element_type=jnp.float32
    )


CHUNK = 1024
MESH = pl.DeviceIdType.MESH


def enter(group, me, devices):
    barrier = pltpu.get_barrier_semaphore()

    def greet(i, carry):
        pl.semaphore_signal(
            barrier, inc=1, device_id=(group, lax.rem(me + i, devices)), device_id_type=MESH
        )
        return carry

    lax.fori_loop(1, devices, greet, 0)
    pl.semaphore_wait(barrier, devices - 1)


def picks(slots, start, rows):
    tokens = slots.shape[1]
    number = lax.broadcasted_iota(jnp.int32, (rows, tokens), 0) + start
    return jnp.where(number == slots, 1.0, 0.0).astype(jnp.bfloat16)


def chunks_of(rows):
    return [(start, min(CHUNK, rows - start)) for start in range(0, rows, CHUNK)]


def fetch_kernel(
    devices, req, tab, wk, wv, weights, replies, wanted, out_rows,
    ring_send, ring_recv, core_send, core_recv, req_send, req_recv, rep_send, rep_recv, own_sem,
):
    group, me = lax.axis_index("groups"), lax.axis_index("table")
    chips = devices // 2
    half_ring = chips // 2
    core, chip = me % 2, me // 2
    odd = chip % 2
    pos = (1 - odd) * (chip // 2) + odd * (chips - 1 - chip // 2)

    def at_ring(r):
        r = (r + 2 * chips) % chips
        late = r // half_ring
        return ((1 - late) * (2 * r) + late * (2 * (chips - 1 - r) + 1)) * 2 + core

    partner = me + 1 - 2 * core
    ways = (at_ring(pos + 1), at_ring(pos - 1))
    half = wk.shape[1] // 2
    parts = (wk, wv)

    def block(d, kv, origin):
        return weights.at[kv, origin, :, pl.ds(d * half, half)]

    def ring_copy(d, kv, s):
        sign = 1 - 2 * d
        origin = at_ring(pos - sign * s)
        source = parts[kv].at[:, pl.ds(d * half, half)] if s == 0 else block(d, kv, origin)
        return pltpu.make_async_remote_copy(
            src_ref=source, dst_ref=block(d, kv, origin),
            send_sem=ring_send.at[d, kv, s], recv_sem=ring_recv.at[d, kv, s],
            device_id=(group, ways[d]), device_id_type=MESH,
        )

    def core_copy(d, kv, s):
        sign = 1 - 2 * d
        origin = at_ring(pos - sign * s)
        source = parts[kv].at[:, pl.ds(d * half, half)] if s == 0 else block(d, kv, origin)
        return pltpu.make_async_remote_copy(
            src_ref=source, dst_ref=block(d, kv, origin),
            send_sem=core_send.at[d, kv, s], recv_sem=core_recv.at[d, kv, s],
            device_id=(group, partner), device_id_type=MESH,
        )

    def own_copy(kv):
        return pltpu.make_async_copy(parts[kv], weights.at[kv, me], own_sem.at[kv])

    def req_copy(i):
        to = lax.rem(me + i, devices)
        return pltpu.make_async_remote_copy(
            src_ref=req.at[to], dst_ref=wanted.at[me],
            send_sem=req_send.at[i], recv_sem=req_recv.at[i],
            device_id=(group, to), device_id_type=MESH,
        )

    def rep_copy(i):
        to = lax.rem(me - i + devices, devices)
        return pltpu.make_async_remote_copy(
            src_ref=out_rows.at[to], dst_ref=replies.at[me],
            send_sem=rep_send.at[i], recv_sem=rep_recv.at[i],
            device_id=(group, to), device_id_type=MESH,
        )

    enter(group, me, devices)

    def send_request(i, carry):
        req_copy(i).start()
        return carry

    lax.fori_loop(1, devices, send_request, 0)
    for kv in range(2):
        for d in range(2):
            ring_copy(d, kv, 0).start()
    for kv in range(2):
        own_copy(kv).start()
        for d in range(2):
            core_copy(d, kv, 0).start()

    def pass_on(s):
        for kv in range(2):
            for d in range(2):
                ring_copy(d, kv, s).wait_recv()
                if s < chips - 2:
                    ring_copy(d, kv, s + 1).start()
                core_copy(d, kv, s + 1).start()

    def look_up(slots):
        total = None
        for start, rows in chunks_of(tab.shape[1]):
            term = jnp.dot(
                tab[:, start : start + rows], picks(slots, start, rows),
                preferred_element_type=jnp.float32,
            )
            total = term if total is None else total + term
        return total.astype(jnp.bfloat16)

    def answer(i, carry):
        req_copy(i).wait_recv()
        source = lax.rem(me - i + devices, devices)
        out_rows[source] = look_up(wanted[source])
        rep_copy(i).start()
        return carry

    first, second = devices * 3 // 8, devices * 3 // 4
    lax.fori_loop(1, first, answer, 0)
    pass_on(0)
    lax.fori_loop(first, second, answer, 0)
    pass_on(1)
    lax.fori_loop(second, devices, answer, 0)
    wanted[me] = req[me]
    replies[me] = look_up(req[me])
    for s in range(2, chips - 1):
        pass_on(s)

    def finish(i, carry):
        req_copy(i).wait_send()
        rep_copy(i).wait_send()
        rep_copy(i).wait_recv()
        return carry

    lax.fori_loop(1, devices, finish, 0)
    for kv in range(2):
        own_copy(kv).wait()
        for d in range(2):
            for s in range(chips):
                if s < chips - 1:
                    ring_copy(d, kv, s).wait_send()
                core_copy(d, kv, s).wait_send()
                core_copy(d, kv, s).wait_recv()


def fetch(requests, table_t, w_key, w_value):
    devices, _, tokens = requests.shape
    row_width = table_t.shape[0]
    chips = devices // 2
    vmem = pl.BlockSpec(memory_space=pltpu.VMEM)
    hbm = pl.BlockSpec(memory_space=pl.ANY)
    dma = pltpu.SemaphoreType.DMA
    return pl.pallas_call(
        functools.partial(fetch_kernel, devices),
        out_shape=(
            jax.ShapeDtypeStruct((2, devices) + w_key.shape, jnp.bfloat16),
            jax.ShapeDtypeStruct((devices, row_width, tokens), jnp.bfloat16),
            jax.ShapeDtypeStruct((devices, 1, tokens), jnp.int32),
        ),
        in_specs=[vmem, vmem, hbm, hbm],
        out_specs=(hbm, vmem, vmem),
        scratch_shapes=[
            pltpu.VMEM((devices, row_width, tokens), jnp.bfloat16),
            dma((2, 2, chips)), dma((2, 2, chips)), dma((2, 2, chips)), dma((2, 2, chips)),
            dma((devices,)), dma((devices,)), dma((devices,)), dma((devices,)), dma((2,)),
        ],
        compiler_params=pltpu.CompilerParams(
            collective_id=0, has_side_effects=True, vmem_limit_bytes=48 * 1024 * 1024
        ),
        name="fetch",
    )(requests, table_t, w_key, w_value)


def return_kernel(devices, out_grads, wanted, result, total, arrived, send, recv):
    group, me = lax.axis_index("groups"), lax.axis_index("table")

    def grad_copy(i):
        to = lax.rem(me + i, devices)
        return pltpu.make_async_remote_copy(
            src_ref=out_grads.at[to], dst_ref=arrived.at[me],
            send_sem=send.at[i], recv_sem=recv.at[i],
            device_id=(group, to), device_id_type=MESH,
        )

    enter(group, me, devices)

    def send_one(i, carry):
        grad_copy(i).start()
        return carry

    lax.fori_loop(1, devices, send_one, 0)

    def add(grads, slots, first):
        for start, rows in chunks_of(total.shape[1]):
            term = lax.dot_general(
                grads, picks(slots, start, rows), (((1,), (1,)), ((), ())),
                preferred_element_type=jnp.float32,
            )
            if first:
                total[:, start : start + rows] = term
            else:
                total[:, start : start + rows] += term

    add(out_grads[me], wanted[me], True)

    def take(i, carry):
        grad_copy(i).wait_recv()
        source = lax.rem(me - i + devices, devices)
        add(arrived[source], wanted[source], False)
        return carry

    lax.fori_loop(1, devices, take, 0)
    for start, rows in chunks_of(total.shape[1]):
        result[:, start : start + rows] = total[:, start : start + rows].astype(jnp.bfloat16)

    def finish(i, carry):
        grad_copy(i).wait_send()
        return carry

    lax.fori_loop(1, devices, finish, 0)


def return_grads(out_grads, wanted, rows):
    devices, row_width, tokens = out_grads.shape
    vmem = pl.BlockSpec(memory_space=pltpu.VMEM)
    dma = pltpu.SemaphoreType.DMA
    return pl.pallas_call(
        functools.partial(return_kernel, devices),
        out_shape=jax.ShapeDtypeStruct((row_width, rows), jnp.bfloat16),
        in_specs=[vmem, vmem],
        out_specs=vmem,
        scratch_shapes=[
            pltpu.VMEM((row_width, rows), jnp.float32),
            pltpu.VMEM((devices, row_width, tokens), jnp.bfloat16),
            dma((devices,)), dma((devices,)),
        ],
        compiler_params=pltpu.CompilerParams(
            collective_id=1, has_side_effects=True, vmem_limit_bytes=48 * 1024 * 1024
        ),
        name="return_grads",
    )(out_grads, wanted)


def on_device(hidden, cotangent, row_owner, row_slot, ngram_table, w_key, w_value, conv_weight):
    tokens_here, heads = row_owner.shape
    row_width = ngram_table.shape[1]
    width = hidden.shape[1]
    devices = lax.axis_size("table")
    owner_t, slot_t = row_owner.T, row_slot.T
    owners = jnp.arange(devices, dtype=jnp.int32)[:, None, None]
    requests = jnp.max(jnp.where(owner_t[None] == owners, slot_t[None], -1), axis=1, keepdims=True)
    gathered, replies, wanted_row_list = fetch(requests, ngram_table.T, w_key, w_value)
    whole = gathered.reshape(2, -1, width)
    memory_t = jnp.zeros((heads, row_width, tokens_here), jnp.bfloat16)
    for owner in range(devices):
        memory_t = jnp.where((owner_t == owner)[:, None, :], replies[owner][None], memory_t)
    memory_t = memory_t.reshape(heads * row_width, tokens_here)
    keys_proj = contract_first(memory_t, whole[0])
    values_proj = contract_first(memory_t, whole[1])
    hidden_f = hidden.astype(jnp.float32)
    hidden_scale_factor = inverse_rms(hidden_f)
    scale_keys = inverse_rms(keys_proj)
    hidden_n = hidden_f * hidden_scale_factor
    keys_n = keys_proj * scale_keys
    root_width = math.sqrt(width)
    score = jnp.sum(hidden_n * keys_n, axis=-1, keepdims=True) / root_width
    gate = jax.nn.sigmoid(score)
    gated = gate * values_proj
    scale_gated = inverse_rms(gated)
    normed = (gated * scale_gated).astype(jnp.bfloat16)
    kernel_taps = conv_weight.shape[0]
    border_rows = (kernel_taps - 1) * MAX_GRAM_ORDER
    window = LENGTH
    position = (
        lax.axis_index("table") * tokens_here + jnp.arange(tokens_here, dtype=jnp.int32)
    ) % window
    before_rows = shifted(normed[tokens_here - border_rows :], "table", 1)
    extended = jnp.concatenate([before_rows, normed], axis=0)
    mixed = jnp.zeros((tokens_here, width), jnp.float32)
    for kernel_tap_index in range(kernel_taps):
        start_offset = kernel_tap_index * MAX_GRAM_ORDER
        moved = extended[
            border_rows - start_offset : border_rows - start_offset + tokens_here
        ].astype(jnp.float32)
        mixed = mixed + conv_weight[kernel_tap_index] * jnp.where(
            (position >= start_offset)[:, None], moved, 0.0
        )
    layer_out = (jax.nn.silu(mixed) + gated).astype(jnp.bfloat16)
    upstream = cotangent.astype(jnp.float32)
    sigm = jax.nn.sigmoid(mixed)
    slope = upstream * sigm * (1.0 + mixed * (1.0 - sigm))
    after_rows = shifted(slope[:border_rows], "table", -1)
    following = jnp.concatenate([slope, after_rows], axis=0)
    normed_grad = jnp.zeros((tokens_here, width), jnp.float32)
    for kernel_tap_index in range(kernel_taps):
        start_offset = kernel_tap_index * MAX_GRAM_ORDER
        moved = following[start_offset : start_offset + tokens_here]
        normed_grad = normed_grad + conv_weight[kernel_tap_index] * jnp.where(
            (position + start_offset < window)[:, None], moved, 0.0
        )
    gated_grad = (
        upstream
        + scale_gated * normed_grad
        - scale_gated**3 * gated * jnp.sum(normed_grad * gated, axis=-1, keepdims=True) / width
    )
    values_grad = (gate * gated_grad).astype(jnp.bfloat16)
    score_grad = jnp.sum(gated_grad * values_proj, axis=-1, keepdims=True) * gate * (1.0 - gate)
    keys_n_grad = score_grad * hidden_n / root_width
    hidden_n_grad = score_grad * keys_n / root_width
    keys_grad = (
        scale_keys * keys_n_grad
        - scale_keys**3
        * keys_proj
        * jnp.sum(keys_n_grad * keys_proj, axis=-1, keepdims=True)
        / width
    ).astype(jnp.bfloat16)
    hidden_grad = (
        hidden_scale_factor * hidden_n_grad
        - hidden_scale_factor**3
        * hidden_f
        * jnp.sum(hidden_n_grad * hidden_f, axis=-1, keepdims=True)
        / width
    ).astype(jnp.bfloat16)
    memory_grad_t = contract_last(whole[0], keys_grad) + contract_last(whole[1], values_grad)
    memory_grad_t = memory_grad_t.astype(jnp.bfloat16).reshape(heads, row_width, tokens_here)
    outgoing = jnp.zeros((devices, row_width, tokens_here), jnp.bfloat16)
    for head in range(heads):
        outgoing = jnp.where(owner_t[head] == owners, memory_grad_t[head][None], outgoing)
    table_grad_t = return_grads(outgoing, wanted_row_list, ngram_table.shape[0])
    return (layer_out, hidden_grad, table_grad_t.T)


def solution(mesh):
    in_specs = (
        P(("groups", "table"), None),
        P(("groups", "table"), None),
        P(("groups", "table"), None),
        P(("groups", "table"), None),
        P("table", None),
        P("table", None),
        P("table", None),
        P(),
    )
    out_specs = (
        P(("groups", "table"), None),
        P(("groups", "table"), None),
        P(("groups", "table"), None),
    )
    return jax.shard_map(
        on_device, mesh=mesh, in_specs=in_specs, out_specs=out_specs, check_vma=False
    )
```

```python
import functools
import math

import jax
import jax.numpy as jnp
from jax import lax
from jax.experimental import pallas as pl
from jax.experimental.pallas import tpu as pltpu
from jax.sharding import PartitionSpec as P

LENGTH = 4096
MAX_GRAM_ORDER = 3


epsilon = 1e-06


def shifted(value, axis, by):
    peers = lax.axis_size(axis)
    pairs = [(i, i + by) for i in range(peers) if 0 <= i + by < peers]
    return lax.ppermute(value, axis, pairs)


def inverse_rms(values):
    return lax.rsqrt(jnp.mean(values * values, axis=-1, keepdims=True) + epsilon)


def contract_last(left, right):
    return lax.dot_general(
        left, right, (((1,), (1,)), ((), ())), preferred_element_type=jnp.float32
    )


def contract_first(left, right):
    return lax.dot_general(
        left, right, (((0,), (0,)), ((), ())), preferred_element_type=jnp.float32
    )


CHUNK = 1024
MESH = pl.DeviceIdType.MESH


def enter(group, me, devices, twin=None):
    barrier = pltpu.get_barrier_semaphore()

    def greet(i, carry):
        pl.semaphore_signal(
            barrier, inc=1, device_id=(group, lax.rem(me + i, devices)), device_id_type=MESH
        )
        return carry

    lax.fori_loop(1, devices, greet, 0)
    if twin is not None:
        pl.semaphore_signal(barrier, inc=1, device_id=(twin, me), device_id_type=MESH)
    pl.semaphore_wait(barrier, devices - 1 if twin is None else devices)


def picks(slots, start, rows):
    tokens = slots.shape[1]
    number = lax.broadcasted_iota(jnp.int32, (rows, tokens), 0) + start
    return jnp.where(number == slots, 1.0, 0.0).astype(jnp.bfloat16)


def chunks_of(rows):
    return [(start, min(CHUNK, rows - start)) for start in range(0, rows, CHUNK)]


def fetch_kernel(
    devices, req, tab_hbm, wk, wv, weights, replies, wanted, tab, out_rows,
    ring_send, ring_recv, core_send, core_recv, twin_send, twin_recv,
    req_send, req_recv, rep_send, rep_recv, own_sem,
):
    group, me = lax.axis_index("groups"), lax.axis_index("table")
    chips = devices // 2
    half_ring = chips // 2
    core, chip = me % 2, me // 2
    odd = chip % 2
    pos = (1 - odd) * (chip // 2) + odd * (chips - 1 - chip // 2)
    mine = group % 2
    twin = group + 1 - 2 * mine

    def at_ring(r):
        r = (r + 2 * chips) % chips
        late = r // half_ring
        return ((1 - late) * (2 * r) + late * (2 * (chips - 1 - r) + 1)) * 2 + core

    partner = me + 1 - 2 * core
    ways = (at_ring(pos + 1), at_ring(pos - 1))
    half = wk.shape[1] // 2

    def block(d, kv, s):
        origin = at_ring(pos - (1 - 2 * d) * s)
        return weights.at[kv, origin, :, pl.ds(d * half, half)]

    def block_copy(ref, send_sem, recv_sem, to):
        return pltpu.make_async_remote_copy(
            src_ref=ref, dst_ref=ref, send_sem=send_sem, recv_sem=recv_sem,
            device_id=to, device_id_type=MESH,
        )

    def ring_copy(d, s):
        return block_copy(
            block(d, mine, s), ring_send.at[d, s], ring_recv.at[d, s], (group, ways[d])
        )

    def twin_copy(d, s):
        return block_copy(
            block(d, mine, s), twin_send.at[d, s], twin_recv.at[d, s], (twin, me)
        )

    def core_copy(d, other, s):
        kv = 1 - mine if other else mine
        return block_copy(
            block(d, kv, s), core_send.at[d, other, s], core_recv.at[d, other, s],
            (group, partner),
        )

    def own_copy(kv):
        return pltpu.make_async_copy((wk, wv)[kv], weights.at[kv, me], own_sem.at[kv])

    def tab_copy():
        return pltpu.make_async_copy(tab_hbm, tab, own_sem.at[2])

    def req_copy(i):
        to = lax.rem(me + i, devices)
        return pltpu.make_async_remote_copy(
            src_ref=req.at[to], dst_ref=wanted.at[me],
            send_sem=req_send.at[i], recv_sem=req_recv.at[i],
            device_id=(group, to), device_id_type=MESH,
        )

    def rep_copy(i):
        to = lax.rem(me - i + devices, devices)
        return pltpu.make_async_remote_copy(
            src_ref=out_rows.at[to], dst_ref=replies.at[me],
            send_sem=rep_send.at[i], recv_sem=rep_recv.at[i],
            device_id=(group, to), device_id_type=MESH,
        )

    for kv in range(2):
        own_copy(kv).start()
    tab_copy().start()
    enter(group, me, devices, twin)

    def send_request(i, carry):
        req_copy(i).start()
        return carry

    lax.fori_loop(1, devices, send_request, 0)
    for kv in range(2):
        own_copy(kv).wait()
    for d in range(2):
        ring_copy(d, 0).start()
    for d in range(2):
        for other in range(2):
            core_copy(d, other, 0).start()
    tab_copy().wait()

    def pass_on(s):
        for d in range(2):
            ring_copy(d, s).wait_recv()
            if s < chips - 2:
                ring_copy(d, s + 1).start()
            twin_copy(d, s + 1).start()
            core_copy(d, 0, s + 1).start()

    def share(s):
        for d in range(2):
            twin_copy(d, s).wait_recv()
            core_copy(d, 1, s).start()

    def look_up(slots):
        total = None
        for start, rows in chunks_of(tab.shape[1]):
            term = jnp.dot(
                tab[:, start : start + rows], picks(slots, start, rows),
                preferred_element_type=jnp.float32,
            )
            total = term if total is None else total + term
        return total.astype(jnp.bfloat16)

    def answer(i, carry):
        req_copy(i).wait_recv()
        source = lax.rem(me - i + devices, devices)
        out_rows[source] = look_up(wanted[source])
        rep_copy(i).start()
        return carry

    bounds = [1] + [devices * j // 4 for j in range(1, 5)]
    stages = min(4, chips - 1)
    for j in range(4):
        lax.fori_loop(bounds[j], bounds[j + 1], answer, 0)
        if j < 3 and j < stages - 1:
            pass_on(j)
    pass_on(stages - 1)
    wanted[me] = req[me]
    replies[me] = look_up(req[me])
    shared = 1
    for s in range(stages, chips - 1):
        pass_on(s)
        share(shared)
        shared += 1
    for s in range(shared, chips):
        share(s)

    def finish(i, carry):
        req_copy(i).wait_send()
        rep_copy(i).wait_send()
        rep_copy(i).wait_recv()
        return carry

    lax.fori_loop(1, devices, finish, 0)
    for d in range(2):
        for s in range(chips):
            if s < chips - 1:
                ring_copy(d, s).wait_send()
            if s > 0:
                twin_copy(d, s).wait_send()
            for other in range(2):
                core_copy(d, other, s).wait_send()
                core_copy(d, other, s).wait_recv()


def fetch(requests, table_t, w_key, w_value):
    devices, _, tokens = requests.shape
    row_width = table_t.shape[0]
    chips = devices // 2
    vmem = pl.BlockSpec(memory_space=pltpu.VMEM)
    hbm = pl.BlockSpec(memory_space=pl.ANY)
    dma = pltpu.SemaphoreType.DMA
    return pl.pallas_call(
        functools.partial(fetch_kernel, devices),
        out_shape=(
            jax.ShapeDtypeStruct((2, devices) + w_key.shape, jnp.bfloat16),
            jax.ShapeDtypeStruct((devices, row_width, tokens), jnp.bfloat16),
            jax.ShapeDtypeStruct((devices, 1, tokens), jnp.int32),
        ),
        in_specs=[vmem, hbm, hbm, hbm],
        out_specs=(hbm, vmem, vmem),
        scratch_shapes=[
            pltpu.VMEM(table_t.shape, jnp.bfloat16),
            pltpu.VMEM((devices, row_width, tokens), jnp.bfloat16),
            dma((2, chips)), dma((2, chips)), dma((2, 2, chips)), dma((2, 2, chips)),
            dma((2, chips)), dma((2, chips)),
            dma((devices,)), dma((devices,)), dma((devices,)), dma((devices,)), dma((3,)),
        ],
        compiler_params=pltpu.CompilerParams(
            collective_id=0, has_side_effects=True, vmem_limit_bytes=48 * 1024 * 1024
        ),
        name="fetch",
    )(requests, table_t, w_key, w_value)


def return_kernel(devices, out_grads, wanted, result, total, arrived, send, recv):
    group, me = lax.axis_index("groups"), lax.axis_index("table")

    def grad_copy(i):
        to = lax.rem(me + i, devices)
        return pltpu.make_async_remote_copy(
            src_ref=out_grads.at[to], dst_ref=arrived.at[me],
            send_sem=send.at[i], recv_sem=recv.at[i],
            device_id=(group, to), device_id_type=MESH,
        )

    enter(group, me, devices)

    def send_one(i, carry):
        grad_copy(i).start()
        return carry

    lax.fori_loop(1, devices, send_one, 0)

    def add(grads, slots, first):
        for start, rows in chunks_of(total.shape[1]):
            term = lax.dot_general(
                grads, picks(slots, start, rows), (((1,), (1,)), ((), ())),
                preferred_element_type=jnp.float32,
            )
            if first:
                total[:, start : start + rows] = term
            else:
                total[:, start : start + rows] += term

    add(out_grads[me], wanted[me], True)

    def take(i, carry):
        grad_copy(i).wait_recv()
        source = lax.rem(me - i + devices, devices)
        add(arrived[source], wanted[source], False)
        return carry

    lax.fori_loop(1, devices, take, 0)
    for start, rows in chunks_of(total.shape[1]):
        result[:, start : start + rows] = total[:, start : start + rows].astype(jnp.bfloat16)

    def finish(i, carry):
        grad_copy(i).wait_send()
        return carry

    lax.fori_loop(1, devices, finish, 0)


def return_grads(out_grads, wanted, rows):
    devices, row_width, tokens = out_grads.shape
    vmem = pl.BlockSpec(memory_space=pltpu.VMEM)
    dma = pltpu.SemaphoreType.DMA
    return pl.pallas_call(
        functools.partial(return_kernel, devices),
        out_shape=jax.ShapeDtypeStruct((row_width, rows), jnp.bfloat16),
        in_specs=[vmem, vmem],
        out_specs=vmem,
        scratch_shapes=[
            pltpu.VMEM((row_width, rows), jnp.float32),
            pltpu.VMEM((devices, row_width, tokens), jnp.bfloat16),
            dma((devices,)), dma((devices,)),
        ],
        compiler_params=pltpu.CompilerParams(
            collective_id=1, has_side_effects=True, vmem_limit_bytes=48 * 1024 * 1024
        ),
        name="return_grads",
    )(out_grads, wanted)


def on_device(hidden, cotangent, row_owner, row_slot, ngram_table, w_key, w_value, conv_weight):
    tokens_here, heads = row_owner.shape
    row_width = ngram_table.shape[1]
    width = hidden.shape[1]
    devices = lax.axis_size("table")
    owner_t, slot_t = row_owner.T, row_slot.T
    owners = jnp.arange(devices, dtype=jnp.int32)[:, None, None]
    requests = jnp.max(jnp.where(owner_t[None] == owners, slot_t[None], -1), axis=1, keepdims=True)
    gathered, replies, wanted_row_list = fetch(requests, ngram_table.T, w_key, w_value)
    whole = gathered.reshape(2, -1, width)
    memory_t = jnp.zeros((heads, row_width, tokens_here), jnp.bfloat16)
    for owner in range(devices):
        memory_t = jnp.where((owner_t == owner)[:, None, :], replies[owner][None], memory_t)
    memory_t = memory_t.reshape(heads * row_width, tokens_here)
    keys_proj = contract_first(memory_t, whole[0])
    values_proj = contract_first(memory_t, whole[1])
    hidden_f = hidden.astype(jnp.float32)
    hidden_scale_factor = inverse_rms(hidden_f)
    scale_keys = inverse_rms(keys_proj)
    hidden_n = hidden_f * hidden_scale_factor
    keys_n = keys_proj * scale_keys
    root_width = math.sqrt(width)
    score = jnp.sum(hidden_n * keys_n, axis=-1, keepdims=True) / root_width
    gate = jax.nn.sigmoid(score)
    gated = gate * values_proj
    scale_gated = inverse_rms(gated)
    normed = (gated * scale_gated).astype(jnp.bfloat16)
    kernel_taps = conv_weight.shape[0]
    border_rows = (kernel_taps - 1) * MAX_GRAM_ORDER
    window = LENGTH
    position = (
        lax.axis_index("table") * tokens_here + jnp.arange(tokens_here, dtype=jnp.int32)
    ) % window
    before_rows = shifted(normed[tokens_here - border_rows :], "table", 1)
    extended = jnp.concatenate([before_rows, normed], axis=0)
    mixed = jnp.zeros((tokens_here, width), jnp.float32)
    for kernel_tap_index in range(kernel_taps):
        start_offset = kernel_tap_index * MAX_GRAM_ORDER
        moved = extended[
            border_rows - start_offset : border_rows - start_offset + tokens_here
        ].astype(jnp.float32)
        mixed = mixed + conv_weight[kernel_tap_index] * jnp.where(
            (position >= start_offset)[:, None], moved, 0.0
        )
    layer_out = (jax.nn.silu(mixed) + gated).astype(jnp.bfloat16)
    upstream = cotangent.astype(jnp.float32)
    sigm = jax.nn.sigmoid(mixed)
    slope = upstream * sigm * (1.0 + mixed * (1.0 - sigm))
    after_rows = shifted(slope[:border_rows], "table", -1)
    following = jnp.concatenate([slope, after_rows], axis=0)
    normed_grad = jnp.zeros((tokens_here, width), jnp.float32)
    for kernel_tap_index in range(kernel_taps):
        start_offset = kernel_tap_index * MAX_GRAM_ORDER
        moved = following[start_offset : start_offset + tokens_here]
        normed_grad = normed_grad + conv_weight[kernel_tap_index] * jnp.where(
            (position + start_offset < window)[:, None], moved, 0.0
        )
    gated_grad = (
        upstream
        + scale_gated * normed_grad
        - scale_gated**3 * gated * jnp.sum(normed_grad * gated, axis=-1, keepdims=True) / width
    )
    values_grad = (gate * gated_grad).astype(jnp.bfloat16)
    score_grad = jnp.sum(gated_grad * values_proj, axis=-1, keepdims=True) * gate * (1.0 - gate)
    keys_n_grad = score_grad * hidden_n / root_width
    hidden_n_grad = score_grad * keys_n / root_width
    keys_grad = (
        scale_keys * keys_n_grad
        - scale_keys**3
        * keys_proj
        * jnp.sum(keys_n_grad * keys_proj, axis=-1, keepdims=True)
        / width
    ).astype(jnp.bfloat16)
    hidden_grad = (
        hidden_scale_factor * hidden_n_grad
        - hidden_scale_factor**3
        * hidden_f
        * jnp.sum(hidden_n_grad * hidden_f, axis=-1, keepdims=True)
        / width
    ).astype(jnp.bfloat16)
    memory_grad_t = contract_last(whole[0], keys_grad) + contract_last(whole[1], values_grad)
    memory_grad_t = memory_grad_t.astype(jnp.bfloat16).reshape(heads, row_width, tokens_here)
    outgoing = jnp.zeros((devices, row_width, tokens_here), jnp.bfloat16)
    for head in range(heads):
        outgoing = jnp.where(owner_t[head] == owners, memory_grad_t[head][None], outgoing)
    table_grad_t = return_grads(outgoing, wanted_row_list, ngram_table.shape[0])
    return (layer_out, hidden_grad, table_grad_t.T)


def solution(mesh):
    in_specs = (
        P(("groups", "table"), None),
        P(("groups", "table"), None),
        P(("groups", "table"), None),
        P(("groups", "table"), None),
        P("table", None),
        P("table", None),
        P("table", None),
        P(),
    )
    out_specs = (
        P(("groups", "table"), None),
        P(("groups", "table"), None),
        P(("groups", "table"), None),
    )
    return jax.shard_map(
        on_device, mesh=mesh, in_specs=in_specs, out_specs=out_specs, check_vma=False
    )
```

```python
import functools
import math

import jax
import jax.numpy as jnp
from jax import lax
from jax.experimental import pallas as pl
from jax.experimental.pallas import tpu as pltpu
from jax.sharding import PartitionSpec as P

LENGTH = 4096
MAX_GRAM_ORDER = 3


epsilon = 1e-06


def shifted(value, axis, by):
    peers = lax.axis_size(axis)
    pairs = [(i, i + by) for i in range(peers) if 0 <= i + by < peers]
    return lax.ppermute(value, axis, pairs)


def inverse_rms(values):
    return lax.rsqrt(jnp.mean(values * values, axis=-1, keepdims=True) + epsilon)


def contract_last(left, right):
    return lax.dot_general(
        left, right, (((1,), (1,)), ((), ())), preferred_element_type=jnp.float32
    )


def contract_first(left, right):
    return lax.dot_general(
        left, right, (((0,), (0,)), ((), ())), preferred_element_type=jnp.float32
    )


CHUNK = 1024
MESH = pl.DeviceIdType.MESH


def enter(group, me, devices, twin=None):
    barrier = pltpu.get_barrier_semaphore()

    def greet(i, carry):
        pl.semaphore_signal(
            barrier, inc=1, device_id=(group, lax.rem(me + i, devices)), device_id_type=MESH
        )
        return carry

    lax.fori_loop(1, devices, greet, 0)
    if twin is not None:
        pl.semaphore_signal(barrier, inc=1, device_id=(twin, me), device_id_type=MESH)
    pl.semaphore_wait(barrier, devices - 1 if twin is None else devices)


def picks(slots, start, rows):
    tokens = slots.shape[1]
    number = lax.broadcasted_iota(jnp.int32, (rows, tokens), 0) + start
    return jnp.where(number == slots, 1.0, 0.0).astype(jnp.bfloat16)


def chunks_of(rows):
    return [(start, min(CHUNK, rows - start)) for start in range(0, rows, CHUNK)]


def fetch_kernel(
    devices, req, tab_hbm, wk, wv, weights, replies, wanted, tab, out_rows,
    ring_send, ring_recv, core_send, core_recv, twin_send, twin_recv,
    req_send, req_recv, rep_send, rep_recv, own_sem,
):
    group, me = lax.axis_index("groups"), lax.axis_index("table")
    chips = devices // 2
    half_ring = chips // 2
    core, chip = me % 2, me // 2
    odd = chip % 2
    pos = (1 - odd) * (chip // 2) + odd * (chips - 1 - chip // 2)
    mine = group % 2
    twin = group + 1 - 2 * mine

    def at_ring(r):
        r = (r + 2 * chips) % chips
        late = r // half_ring
        return ((1 - late) * (2 * r) + late * (2 * (chips - 1 - r) + 1)) * 2 + core

    partner = me + 1 - 2 * core
    ways = (at_ring(pos + 1), at_ring(pos - 1))
    half = wk.shape[1] // 2

    def block(d, kv, s):
        origin = at_ring(pos - (1 - 2 * d) * s)
        return weights.at[kv, origin, :, pl.ds(d * half, half)]

    def block_copy(ref, send_sem, recv_sem, to):
        return pltpu.make_async_remote_copy(
            src_ref=ref, dst_ref=ref, send_sem=send_sem, recv_sem=recv_sem,
            device_id=to, device_id_type=MESH,
        )

    def ring_copy(d, s):
        return block_copy(
            block(d, mine, s), ring_send.at[d, s], ring_recv.at[d, s], (group, ways[d])
        )

    def twin_copy(d, s):
        return block_copy(
            block(d, mine, s), twin_send.at[d, s], twin_recv.at[d, s], (twin, me)
        )

    def core_copy(d, other, s):
        kv = 1 - mine if other else mine
        return block_copy(
            block(d, kv, s), core_send.at[d, other, s], core_recv.at[d, other, s],
            (group, partner),
        )

    def own_copy(kv):
        return pltpu.make_async_copy((wk, wv)[kv], weights.at[kv, me], own_sem.at[kv])

    def tab_copy():
        return pltpu.make_async_copy(tab_hbm, tab, own_sem.at[2])

    def req_copy(i):
        to = lax.rem(me + i, devices)
        return pltpu.make_async_remote_copy(
            src_ref=req.at[to], dst_ref=wanted.at[me],
            send_sem=req_send.at[i], recv_sem=req_recv.at[i],
            device_id=(group, to), device_id_type=MESH,
        )

    def rep_copy(i):
        to = lax.rem(me - i + devices, devices)
        return pltpu.make_async_remote_copy(
            src_ref=out_rows.at[to], dst_ref=replies.at[me],
            send_sem=rep_send.at[i], recv_sem=rep_recv.at[i],
            device_id=(group, to), device_id_type=MESH,
        )

    for kv in range(2):
        own_copy(kv).start()
    tab_copy().start()
    enter(group, me, devices, twin)

    def send_request(i, carry):
        req_copy(i).start()
        return carry

    lax.fori_loop(1, devices, send_request, 0)
    for kv in range(2):
        own_copy(kv).wait()
    for d in range(2):
        ring_copy(d, 0).start()
    for d in range(2):
        for other in range(2):
            core_copy(d, other, 0).start()
    tab_copy().wait()

    def pass_on(s):
        for d in range(2):
            ring_copy(d, s).wait_recv()
            if s < chips - 2:
                ring_copy(d, s + 1).start()
            twin_copy(d, s + 1).start()
            core_copy(d, 0, s + 1).start()

    def share(s):
        for d in range(2):
            twin_copy(d, s).wait_recv()
            core_copy(d, 1, s).start()

    def look_up(slots):
        total = None
        for start, rows in chunks_of(tab.shape[1]):
            term = jnp.dot(
                tab[:, start : start + rows], picks(slots, start, rows),
                preferred_element_type=jnp.float32,
            )
            total = term if total is None else total + term
        return total.astype(jnp.bfloat16)

    def answer(i, carry):
        req_copy(i).wait_recv()
        source = lax.rem(me - i + devices, devices)
        out_rows[source] = look_up(wanted[source])
        rep_copy(i).start()
        return carry

    bounds = [1] + [devices * j // 8 for j in range(1, 9)]
    passed, shared = 1, 1
    pass_on(0)
    for j in range(8):
        lax.fori_loop(bounds[j], bounds[j + 1], answer, 0)
        if passed < chips - 1:
            pass_on(passed)
            passed += 1
        if j in (3, 5, 7) and shared < passed:
            share(shared)
            shared += 1
    wanted[me] = req[me]
    replies[me] = look_up(req[me])
    for s in range(passed, chips - 1):
        pass_on(s)
        share(shared)
        shared += 1
    for s in range(shared, chips):
        share(s)

    def finish(i, carry):
        req_copy(i).wait_send()
        rep_copy(i).wait_send()
        rep_copy(i).wait_recv()
        return carry

    lax.fori_loop(1, devices, finish, 0)
    for d in range(2):
        for s in range(chips):
            if s < chips - 1:
                ring_copy(d, s).wait_send()
            if s > 0:
                twin_copy(d, s).wait_send()
            for other in range(2):
                core_copy(d, other, s).wait_send()
                core_copy(d, other, s).wait_recv()


def fetch(requests, table_t, w_key, w_value):
    devices, _, tokens = requests.shape
    row_width = table_t.shape[0]
    chips = devices // 2
    vmem = pl.BlockSpec(memory_space=pltpu.VMEM)
    hbm = pl.BlockSpec(memory_space=pl.ANY)
    dma = pltpu.SemaphoreType.DMA
    return pl.pallas_call(
        functools.partial(fetch_kernel, devices),
        out_shape=(
            jax.ShapeDtypeStruct((2, devices) + w_key.shape, jnp.bfloat16),
            jax.ShapeDtypeStruct((devices, row_width, tokens), jnp.bfloat16),
            jax.ShapeDtypeStruct((devices, 1, tokens), jnp.int32),
        ),
        in_specs=[vmem, hbm, hbm, hbm],
        out_specs=(hbm, vmem, vmem),
        scratch_shapes=[
            pltpu.VMEM(table_t.shape, jnp.bfloat16),
            pltpu.VMEM((devices, row_width, tokens), jnp.bfloat16),
            dma((2, chips)), dma((2, chips)), dma((2, 2, chips)), dma((2, 2, chips)),
            dma((2, chips)), dma((2, chips)),
            dma((devices,)), dma((devices,)), dma((devices,)), dma((devices,)), dma((3,)),
        ],
        compiler_params=pltpu.CompilerParams(
            collective_id=0, has_side_effects=True, vmem_limit_bytes=48 * 1024 * 1024
        ),
        name="fetch",
    )(requests, table_t, w_key, w_value)


def return_kernel(devices, out_grads, wanted, result, total, arrived, send, recv):
    group, me = lax.axis_index("groups"), lax.axis_index("table")

    def grad_copy(i):
        to = lax.rem(me + i, devices)
        return pltpu.make_async_remote_copy(
            src_ref=out_grads.at[to], dst_ref=arrived.at[me],
            send_sem=send.at[i], recv_sem=recv.at[i],
            device_id=(group, to), device_id_type=MESH,
        )

    enter(group, me, devices)

    def send_one(i, carry):
        grad_copy(i).start()
        return carry

    lax.fori_loop(1, devices, send_one, 0)

    def add(grads, slots, first):
        for start, rows in chunks_of(total.shape[1]):
            term = lax.dot_general(
                grads, picks(slots, start, rows), (((1,), (1,)), ((), ())),
                preferred_element_type=jnp.float32,
            )
            if first:
                total[:, start : start + rows] = term
            else:
                total[:, start : start + rows] += term

    add(out_grads[me], wanted[me], True)

    def take(i, carry):
        grad_copy(i).wait_recv()
        source = lax.rem(me - i + devices, devices)
        add(arrived[source], wanted[source], False)
        return carry

    lax.fori_loop(1, devices, take, 0)
    for start, rows in chunks_of(total.shape[1]):
        result[:, start : start + rows] = total[:, start : start + rows].astype(jnp.bfloat16)

    def finish(i, carry):
        grad_copy(i).wait_send()
        return carry

    lax.fori_loop(1, devices, finish, 0)


def return_grads(out_grads, wanted, rows):
    devices, row_width, tokens = out_grads.shape
    vmem = pl.BlockSpec(memory_space=pltpu.VMEM)
    dma = pltpu.SemaphoreType.DMA
    return pl.pallas_call(
        functools.partial(return_kernel, devices),
        out_shape=jax.ShapeDtypeStruct((row_width, rows), jnp.bfloat16),
        in_specs=[vmem, vmem],
        out_specs=vmem,
        scratch_shapes=[
            pltpu.VMEM((row_width, rows), jnp.float32),
            pltpu.VMEM((devices, row_width, tokens), jnp.bfloat16),
            dma((devices,)), dma((devices,)),
        ],
        compiler_params=pltpu.CompilerParams(
            collective_id=1, has_side_effects=True, vmem_limit_bytes=48 * 1024 * 1024
        ),
        name="return_grads",
    )(out_grads, wanted)


def on_device(hidden, cotangent, row_owner, row_slot, ngram_table, w_key, w_value, conv_weight):
    tokens_here, heads = row_owner.shape
    row_width = ngram_table.shape[1]
    width = hidden.shape[1]
    devices = lax.axis_size("table")
    owner_t, slot_t = row_owner.T, row_slot.T
    owners = jnp.arange(devices, dtype=jnp.int32)[:, None, None]
    requests = jnp.max(jnp.where(owner_t[None] == owners, slot_t[None], -1), axis=1, keepdims=True)
    gathered, replies, wanted_row_list = fetch(requests, ngram_table.T, w_key, w_value)
    whole = gathered.reshape(2, -1, width)
    memory_t = jnp.zeros((heads, row_width, tokens_here), jnp.bfloat16)
    for owner in range(devices):
        memory_t = jnp.where((owner_t == owner)[:, None, :], replies[owner][None], memory_t)
    memory_t = memory_t.reshape(heads * row_width, tokens_here)
    keys_proj = contract_first(memory_t, whole[0])
    values_proj = contract_first(memory_t, whole[1])
    hidden_f = hidden.astype(jnp.float32)
    hidden_scale_factor = inverse_rms(hidden_f)
    scale_keys = inverse_rms(keys_proj)
    hidden_n = hidden_f * hidden_scale_factor
    keys_n = keys_proj * scale_keys
    root_width = math.sqrt(width)
    score = jnp.sum(hidden_n * keys_n, axis=-1, keepdims=True) / root_width
    gate = jax.nn.sigmoid(score)
    gated = gate * values_proj
    scale_gated = inverse_rms(gated)
    normed = (gated * scale_gated).astype(jnp.bfloat16)
    kernel_taps = conv_weight.shape[0]
    border_rows = (kernel_taps - 1) * MAX_GRAM_ORDER
    window = LENGTH
    position = (
        lax.axis_index("table") * tokens_here + jnp.arange(tokens_here, dtype=jnp.int32)
    ) % window
    before_rows = shifted(normed[tokens_here - border_rows :], "table", 1)
    extended = jnp.concatenate([before_rows, normed], axis=0)
    mixed = jnp.zeros((tokens_here, width), jnp.float32)
    for kernel_tap_index in range(kernel_taps):
        start_offset = kernel_tap_index * MAX_GRAM_ORDER
        moved = extended[
            border_rows - start_offset : border_rows - start_offset + tokens_here
        ].astype(jnp.float32)
        mixed = mixed + conv_weight[kernel_tap_index] * jnp.where(
            (position >= start_offset)[:, None], moved, 0.0
        )
    layer_out = (jax.nn.silu(mixed) + gated).astype(jnp.bfloat16)
    upstream = cotangent.astype(jnp.float32)
    sigm = jax.nn.sigmoid(mixed)
    slope = upstream * sigm * (1.0 + mixed * (1.0 - sigm))
    after_rows = shifted(slope[:border_rows], "table", -1)
    following = jnp.concatenate([slope, after_rows], axis=0)
    normed_grad = jnp.zeros((tokens_here, width), jnp.float32)
    for kernel_tap_index in range(kernel_taps):
        start_offset = kernel_tap_index * MAX_GRAM_ORDER
        moved = following[start_offset : start_offset + tokens_here]
        normed_grad = normed_grad + conv_weight[kernel_tap_index] * jnp.where(
            (position + start_offset < window)[:, None], moved, 0.0
        )
    gated_grad = (
        upstream
        + scale_gated * normed_grad
        - scale_gated**3 * gated * jnp.sum(normed_grad * gated, axis=-1, keepdims=True) / width
    )
    values_grad = (gate * gated_grad).astype(jnp.bfloat16)
    score_grad = jnp.sum(gated_grad * values_proj, axis=-1, keepdims=True) * gate * (1.0 - gate)
    keys_n_grad = score_grad * hidden_n / root_width
    hidden_n_grad = score_grad * keys_n / root_width
    keys_grad = (
        scale_keys * keys_n_grad
        - scale_keys**3
        * keys_proj
        * jnp.sum(keys_n_grad * keys_proj, axis=-1, keepdims=True)
        / width
    ).astype(jnp.bfloat16)
    hidden_grad = (
        hidden_scale_factor * hidden_n_grad
        - hidden_scale_factor**3
        * hidden_f
        * jnp.sum(hidden_n_grad * hidden_f, axis=-1, keepdims=True)
        / width
    ).astype(jnp.bfloat16)
    memory_grad_t = contract_last(whole[0], keys_grad) + contract_last(whole[1], values_grad)
    memory_grad_t = memory_grad_t.astype(jnp.bfloat16).reshape(heads, row_width, tokens_here)
    outgoing = jnp.zeros((devices, row_width, tokens_here), jnp.bfloat16)
    for head in range(heads):
        outgoing = jnp.where(owner_t[head] == owners, memory_grad_t[head][None], outgoing)
    table_grad_t = return_grads(outgoing, wanted_row_list, ngram_table.shape[0])
    return (layer_out, hidden_grad, table_grad_t.T)


def solution(mesh):
    in_specs = (
        P(("groups", "table"), None),
        P(("groups", "table"), None),
        P(("groups", "table"), None),
        P(("groups", "table"), None),
        P("table", None),
        P("table", None),
        P("table", None),
        P(),
    )
    out_specs = (
        P(("groups", "table"), None),
        P(("groups", "table"), None),
        P(("groups", "table"), None),
    )
    return jax.shard_map(
        on_device, mesh=mesh, in_specs=in_specs, out_specs=out_specs, check_vma=False
    )
```
